32 devices in a mesh: rep: 2 (over x), member: 4 (over y, core), tp: 4 (over z).
Axes of the slice: x: 2, y: 2, z: 4, core: 2. Of those that a mesh axis runs over, the one named last changes fastest.
Arguments:
- states: bfloat16 [4096, 1024], P(('rep', 'member', 'tp')), parts along dimension 0, may hold values from -6 to 6
- member_of: int32 [4096, 1], P(('rep', 'member', 'tp')), parts along dimension 0, may hold values from 0 to 1; in each aligned block of 128 rows (0 to 127, 128 to 255, ...) at most 128 rows name the same one
- place: int32 [4096], P(('rep', 'member', 'tp')), parts along dimension 0, may hold values from 0 to 2047, as said below
- norm_gain: float32 [2, 1024], replicated, may hold values from 0.5 to 2
- w_up: bfloat16 [4, 1024, 2048], P('member', None, 'tp'), may hold values from -0.1875 to 0.1875
- w_down: bfloat16 [4, 2048, 1024], P('member', 'tp'), may hold values from -0.09375 to 0.09375
- policy_gain: float32 [1024], replicated, may hold values from 0.5 to 2
- w_policy: bfloat16 [1024, 128], replicated, may hold values from -0.1875 to 0.1875
Outputs:
- imagined: bfloat16 [4096, 1024], P(('rep', 'member', 'tp')), parts along dimension 0
- action: bfloat16 [4096, 128], P(('rep', 'member', 'tp')), parts along dimension 0
The draws below stay inside these ranges and needn't reach their ends.
There are 2 independent parts, one for each index of `rep`. The reference program is written for one: setup_inputs(seed, part) draws one part's arguments, and reference() takes and returns one part's arrays. A program takes and returns all parts, laid end to end along the dimension named above; an argument that names none is the same for every part. Nothing has to cross between parts.
Inputs may be any that keep to these rules, and one draw needn't show every extreme that they name: `member_of`: at most 128 of the rows of one device name any one member, and that count is reached on some device. `place`: A permutation of the 2048 learner positions; learner device k holds positions k * 128 to (k + 1) * 128 - 1, and the rows of each device go exactly 8 to every learner device.
All inputs are finite; a program needn't handle non-finite values.
Results may differ from the reference program's by a relative error of at most 0.0069.
Values may be sent and summed in bfloat16 or wider, within the bound.
A program may use at most 128 MiB of HBM per device.

```python
import math
import jax
import jax.numpy as jnp
import numpy as np
from jax import lax

D = 1024
FF = 4096
ACT = 128
ROW_DEV = 128
MEMBERS = 2
ROWS = 2048
CAPM = 128
REGROUP = 8


def draw_place(key, part):
    sources = ROWS // ROW_DEV
    first_key, second_key = jax.random.split(key)

    def shuffled(inner_key):
        return jax.random.permutation(inner_key, ROW_DEV)
    spread = jax.vmap(shuffled)(jax.random.split(first_key, sources)).astype(jnp.int32)
    learner = spread // REGROUP
    within = spread % REGROUP
    sectioned = jnp.arange(sources, dtype=jnp.int32)[:, None] * REGROUP + within
    shuffle = jax.vmap(shuffled)(jax.random.split(second_key, sources)).astype(jnp.int32)
    final = shuffle[learner, sectioned]
    return (learner * ROW_DEV + final).reshape(-1).astype(jnp.int32)


def block_scale(stream_key, shape, cuts, low, high):
    loudness = 1.0
    for position, shards_of in cuts:
        steps = jax.random.uniform(jax.random.fold_in(jax.random.fold_in(stream_key, 6), position), (shards_of,), jnp.float32, low / len(cuts), high / len(cuts))
        loudness = loudness * jnp.repeat(jnp.exp(steps), shape[position] // shards_of).reshape((-1,) + (1,) * (len(shape) - 1 - position))
    return loudness


def routed_block(rng, own, number, rows, count, top, bound, skew):
    ranking = jax.random.permutation(rng, count)
    packed, ordinary = portions_of(count, rows * top, bound, skew, True), portions_of(count, rows * top, bound, skew, False)
    places = jnp.arange(count)

    def named(sizes, turn):
        used = int((sizes > 0).sum())
        fixed = max(1, used // 4)
        passed = fixed + (places - fixed + turn * (used - fixed)) % max(1, count - fixed)
        return jnp.zeros((count,), jnp.int32).at[ranking[jnp.where(places < fixed, places, passed)]].set(jnp.asarray(sizes, jnp.int32))

    sizes = jnp.where(number % 4 == 0, named(packed, number // 4), named(ordinary, number - number // 4 - 1))
    mixed = jax.random.permutation(jax.random.fold_in(own, 3), count)
    giver, sink = mixed[0:count // 2 * 2:2], mixed[1:count // 2 * 2:2]
    room = jnp.minimum(sizes[giver] - 1, bound - sizes[sink]) // 2
    room = jnp.where((giver == ranking[0]) | (sink == ranking[0]) | (sizes[sink] == 0), 0, jnp.maximum(room, 0))
    passed = jax.random.randint(jax.random.fold_in(own, 4), (count // 2,), 0, 1 << 20) % (room + 1)
    sizes = sizes.at[giver].add(-passed).at[sink].add(passed)
    labels = jnp.searchsorted(jnp.cumsum(sizes), jnp.arange(rows * top), side="right").astype(jnp.int32)
    table = labels.reshape(top, rows).T
    table = table[jax.random.permutation(jax.random.fold_in(own, 1), rows)]
    turn = jax.random.randint(jax.random.fold_in(own, 2), (rows, 1), 0, top)
    return jnp.take_along_axis(table, (jnp.arange(top)[None, :] + turn) % top, axis=1)


def portions_of(number_of, total, bound, skew, full):
    loads = [(1 << 20) // math.isqrt(rank ** skew) + 1 for rank in range(1, number_of + 1)]
    largest = bound if full else min(bound, max(-(-total // number_of), total * loads[0] // sum(loads)))
    least = 1 if total - largest >= number_of - 1 else 0
    holding, surplus = [largest] + [least] * (number_of - 1), total - largest - least * (number_of - 1)
    while surplus > 0:
        candidates = [i for i in range(1, number_of) if holding[i] < largest] or [i for i in range(1, number_of) if holding[i] < bound]
        pool, remaining = sum([loads[i] for i in candidates]), surplus
        for i in candidates:
            addition = min(bound - holding[i], max(1, remaining * loads[i] // pool), surplus)
            holding[i] = holding[i] + addition
            surplus = surplus - addition
    return np.array(holding)


def normal_values(rng, extent, deviation, reach, cuts=(), held_as=jnp.bfloat16):
    array = deviation * jax.random.normal(rng, extent, jnp.float32)
    if cuts:
        array = array * block_scale(rng, extent, cuts, -0.22, 0.18)
    return jnp.clip(array, -reach, reach).astype(held_as)


def setup_inputs(seed: int = 0, part: int = 0) -> dict:
    arg_keys = jax.random.split(jax.random.key(seed), 9)
    part_splits = jax.random.split(jax.random.fold_in(arg_keys[8], part), 9)
    states = normal_values(part_splits[0], (ROWS, D), 1.0, 6.0, ((0, 16),))
    member_of_keys = jax.random.split(jax.random.fold_in(part_splits[1], 1), ROWS // ROW_DEV)
    member_of_turns = jax.random.permutation(jax.random.fold_in(part_splits[1], 3), ROWS // ROW_DEV)
    member_of = jax.vmap(lambda own, number: routed_block(jax.random.fold_in(part_splits[1], 2), own, number, ROW_DEV, MEMBERS, 1, CAPM, 2))(member_of_keys, member_of_turns).reshape((ROWS, 1))
    place = draw_place(jax.random.fold_in(jax.random.fold_in(arg_keys[8], part), 71), part)
    norm_gain = jnp.clip(jnp.exp(jax.random.uniform(arg_keys[3], (MEMBERS, D), jnp.float32, math.log(0.5), math.log(2.0))), 0.5, 2.0)
    w_up = normal_values(arg_keys[4], (2 * MEMBERS, D, FF // 2), D ** -0.5, 0.1875, ((0, 4), (2, 4)))
    w_down = normal_values(arg_keys[5], (2 * MEMBERS, FF // 2, D), FF ** -0.5, 0.09375, ((0, 4), (1, 4)))
    policy_gain = jnp.clip(jnp.exp(jax.random.uniform(arg_keys[6], (D,), jnp.float32, math.log(0.5), math.log(2.0))), 0.5, 2.0)
    w_policy = normal_values(arg_keys[7], (D, ACT), D ** -0.5, 0.1875)
    return {"states": states, "member_of": member_of, "place": place, "norm_gain": norm_gain, "w_up": w_up, "w_down": w_down, "policy_gain": policy_gain, "w_policy": w_policy}


def rms_scale(values, gain):
    mean_square = lax.optimization_barrier(jnp.mean(values * values, axis=-1, keepdims=True))
    return values * lax.rsqrt(mean_square + 1e-06) * gain

def reference(states, member_of, place, norm_gain, w_up, w_down, policy_gain, w_policy):
    member = member_of[:, 0].astype(jnp.int32)
    order = jnp.argsort(member, stable=True).astype(jnp.int32)
    sorted_member = member[order]
    sorted_states = states[order]
    block_rows = min(256, ROWS)
    block_count = ROWS // block_rows

    def one_block(pair):
        block_states, block_member = pair
        base = block_states.astype(jnp.float32)

        def apply_member(member_id, running):
            up_whole = jnp.concatenate([w_up[2 * member_id], w_up[2 * member_id + 1]], axis=1)
            down_whole = jnp.concatenate([w_down[2 * member_id], w_down[2 * member_id + 1]], axis=0)
            normed = rms_scale(base, norm_gain[member_id]).astype(jnp.bfloat16)
            hidden = jax.nn.gelu(jnp.dot(normed, up_whole, preferred_element_type=jnp.float32)).astype(jnp.bfloat16)
            change = jnp.dot(hidden, down_whole, preferred_element_type=jnp.float32)
            return jnp.where((block_member == member_id)[:, None], change, running)
        change = lax.fori_loop(block_member[0], block_member[-1] + 1, apply_member, jnp.zeros(base.shape, jnp.float32))
        return (base + change).astype(jnp.bfloat16)
    predicted = lax.map(one_block, (sorted_states.reshape(block_count, block_rows, D), sorted_member.reshape(block_count, block_rows)))
    predicted = predicted.reshape(ROWS, D)
    imagined = jnp.zeros((ROWS, D), jnp.bfloat16).at[place[order]].set(predicted)
    policy_normed = rms_scale(imagined.astype(jnp.float32), policy_gain).astype(jnp.bfloat16)
    action = jnp.tanh(jnp.dot(policy_normed, w_policy, preferred_element_type=jnp.float32)).astype(jnp.bfloat16)
    return (imagined, action)
```

```python
import jax
import jax.numpy as jnp
from jax import lax
from jax.experimental import pallas as pl
from jax.experimental.pallas import tpu as pltpu
from jax.sharding import PartitionSpec as P


def from_partner(value, axis, distance):
    return lax.ppermute(value, axis, [(i, i ^ 1 << distance) for i in range(lax.axis_size(axis))])


def rms_scale(values, gain):
    mean_square = jnp.mean(values * values, axis=-1, keepdims=True)
    return values * lax.rsqrt(mean_square + 1e-06) * gain


def running_rank(member_hits):
    return jnp.sum((jnp.cumsum(member_hits, axis=0) - member_hits) * member_hits, axis=1)


def dispatched(states, member_of, place, norm_gain, w_up, w_down, policy_gain, w_policy):
    n_member = lax.axis_size("member")
    n_tp = lax.axis_size("tp")
    n_dev = n_member * n_tp
    group_width = 2 * n_tp
    member_total = n_member // 2
    rows_here = states.shape[0]
    feature_width = states.shape[1]
    slot_count = 2 * rows_here // n_dev
    member = member_of[:, 0]
    member_hits = (member[:, None] == jnp.arange(member_total, dtype=jnp.int32)[None, :]).astype(
        jnp.int32
    )
    earlier = running_rank(member_hits)
    target = (member * group_width + earlier % group_width) * slot_count + earlier // group_width
    picker = (jnp.arange(n_dev * slot_count, dtype=jnp.int32)[:, None] == target[None, :]).astype(
        jnp.bfloat16
    )
    outgoing = jnp.dot(picker, states, preferred_element_type=jnp.float32).astype(jnp.bfloat16)
    arrived = lax.all_to_all(
        outgoing.reshape(n_dev, slot_count, feature_width),
        ("member", "tp"),
        split_axis=0,
        concat_axis=0,
        tiled=True,
    )
    arrived = arrived.reshape(n_dev * slot_count, feature_width)
    arrived_count = arrived.shape[0]
    own_member = lax.axis_index("member") // 2
    gain_here = lax.dynamic_index_in_dim(norm_gain, own_member, 0, keepdims=False)
    normed = rms_scale(arrived.astype(jnp.float32), gain_here).astype(jnp.bfloat16)
    partner_normed = from_partner(normed, "member", 0)
    both_rows = jnp.concatenate([normed, partner_normed], axis=0)
    up_local = w_up[0]
    down_local = w_down[0]
    hidden = jax.nn.gelu(
        jnp.dot(
            lax.all_gather(both_rows, "tp", axis=0, tiled=True),
            up_local,
            preferred_element_type=jnp.float32,
        )
    ).astype(jnp.bfloat16)
    half_change = lax.psum_scatter(
        jnp.dot(hidden, down_local, preferred_element_type=jnp.float32),
        "tp",
        scatter_dimension=0,
        tiled=True,
    )
    partner_part = from_partner(half_change[arrived_count:], "member", 0)
    change = half_change[:arrived_count] + partner_part
    predicted = (arrived.astype(jnp.float32) + change).astype(jnp.bfloat16)
    returned = lax.all_to_all(
        predicted.reshape(n_dev, slot_count, feature_width),
        ("member", "tp"),
        split_axis=0,
        concat_axis=0,
        tiled=True,
    )
    returned = returned.reshape(n_dev * slot_count, feature_width)
    own_rows = jnp.einsum("sr,sd->rd", picker, returned, preferred_element_type=jnp.float32).astype(
        jnp.bfloat16
    )
    per_learner = rows_here // n_dev
    learner = place // rows_here
    spot_index = place % rows_here
    learner_hits = (learner[:, None] == jnp.arange(n_dev, dtype=jnp.int32)[None, :]).astype(
        jnp.int32
    )
    lane_index = learner * per_learner + running_rank(learner_hits)
    placer = jnp.arange(rows_here, dtype=jnp.int32)[:, None] == lane_index[None, :]
    packed = jnp.dot(
        placer.astype(jnp.bfloat16), own_rows, preferred_element_type=jnp.float32
    ).astype(jnp.bfloat16)
    packed_spot = jnp.sum(placer.astype(jnp.int32) * spot_index[None, :], axis=1)
    arrivals, arrival_spots = (
        lax.all_to_all(
            packed.reshape(n_dev, per_learner, feature_width),
            ("member", "tp"),
            split_axis=0,
            concat_axis=0,
            tiled=True,
        ),
        lax.all_to_all(
            packed_spot.reshape(n_dev, per_learner),
            ("member", "tp"),
            split_axis=0,
            concat_axis=0,
            tiled=True,
        ),
    )
    arrivals = arrivals.reshape(rows_here, feature_width)
    arrival_spots = arrival_spots.reshape(rows_here)
    settle = (jnp.arange(rows_here, dtype=jnp.int32)[:, None] == arrival_spots[None, :]).astype(
        jnp.bfloat16
    )
    imagined = jnp.dot(settle, arrivals, preferred_element_type=jnp.float32).astype(jnp.bfloat16)
    policy_normed = rms_scale(imagined.astype(jnp.float32), policy_gain).astype(jnp.bfloat16)
    action = jnp.tanh(jnp.dot(policy_normed, w_policy, preferred_element_type=jnp.float32)).astype(
        jnp.bfloat16
    )
    return (imagined, action)


RIGHT, LEFT, ACROSS, SIBLING = range(4)


def near_order(z):
    return (
        z,
        z - 1 + 2 * ((3 - z) // 3),
        2 + z // 2 - 2 * (z // 3),
        3 - 3 * (z // 2),
    )


def rollout_kernel(
    states_ref,
    member_ref,
    place_ref,
    gain_ref,
    up_ref,
    down_ref,
    policy_gain_ref,
    policy_ref,
    imagined_ref,
    action_ref,
    rows,
    notes,
    parts,
    sibling_parts,
    sums,
    across_parts,
    from_left,
    from_right,
    outgoing,
    total,
    gather_send,
    gather_recv,
    part_send,
    part_recv,
    across_send,
    across_recv,
    line_send,
    left_recv,
    right_recv,
):
    width = states_ref.shape[1]
    z = lax.axis_index("tp")
    m = lax.axis_index("member")
    y = m // 2
    h = m % 2
    chip = y * 4 + z
    targets = {
        RIGHT: {"tp": z + 1},
        LEFT: {"tp": z - 1},
        ACROSS: {"member": m + 2 - 4 * y},
        SIBLING: {"member": m + 1 - 2 * h},
    }
    has_right = z < 3
    has_left = z > 0
    order = near_order(z)

    def greet(way):
        pl.semaphore_signal(
            barrier, inc=1, device_id=targets[way], device_id_type=pl.DeviceIdType.MESH
        )

    def remote(source, target, send_sem, recv_sem, way):
        return pltpu.make_async_remote_copy(
            src_ref=source,
            dst_ref=target,
            send_sem=send_sem,
            recv_sem=recv_sem,
            device_id=targets[way],
            device_id_type=pl.DeviceIdType.MESH,
        )

    barrier = pltpu.get_barrier_semaphore()
    greet(ACROSS)
    greet(SIBLING)
    pl.when(has_right)(lambda: greet(RIGHT))
    pl.when(has_left)(lambda: greet(LEFT))

    lane = lax.broadcasted_iota(jnp.int32, (128, 128), 1)
    sub = lax.broadcasted_iota(jnp.int32, (128, 128), 0)
    place_row = place_ref[...]
    learner = place_row >> 7
    spot = place_row & 127
    key_row = ((((learner >> 3) << 2) + (learner & 3)) << 1) + ((learner >> 2) & 1)
    rank_row = key_row * 128 + lax.broadcasted_iota(jnp.int32, (1, 128), 1)
    rank_col = jnp.sum(jnp.where(lane == sub, rank_row, 0), axis=1, keepdims=True)
    sorted_row = jnp.sum((rank_col < rank_row).astype(jnp.int32), axis=0, keepdims=True)
    picker = (sub == sorted_row).astype(jnp.bfloat16)
    member_row = jnp.sum(jnp.where(lane == sub, member_ref[...], 0), axis=0, keepdims=True)
    line = lax.broadcasted_iota(jnp.int32, (16, 128), 0)
    facts = jnp.where(line == 0, member_row, jnp.where(line == 1, spot, 0))
    own_notes = lax.dot_general(
        facts.astype(jnp.bfloat16),
        picker,
        (((1,), (1,)), ((), ())),
        preferred_element_type=jnp.float32,
    )
    notes[chip, h] = own_notes[:8]
    rows[chip, h] = jnp.dot(
        picker, states_ref[...], preferred_element_type=jnp.float32
    ).astype(jnp.bfloat16)

    pl.semaphore_wait(barrier, 2 + (z + 2) // 3 + (5 - z) // 3)

    def block(way, at):
        return [
            remote(
                buffer.at[at, h],
                buffer.at[at, h],
                gather_send.at[kind, way, at],
                gather_recv.at[kind, at, h],
                way,
            )
            for kind, buffer in enumerate((notes, rows))
        ]

    def send_block(way, at):
        for copy in block(way, at):
            copy.start()

    def await_block(at, core):
        for kind, buffer in enumerate((notes, rows)):
            remote(
                buffer.at[at, core],
                buffer.at[at, core],
                gather_send.at[kind, SIBLING, at],
                gather_recv.at[kind, at, core],
                SIBLING,
            ).wait_recv()

    gain = gain_ref[pl.ds(y, 1), :]

    def part(at):
        return remote(
            parts.at[at, 1 - h],
            sibling_parts.at[at],
            part_send.at[at],
            part_recv.at[at],
            SIBLING,
        )

    def predict(at):
        base = jnp.concatenate([rows[at, 0], rows[at, 1]], axis=0).astype(jnp.float32)
        kept = jnp.concatenate(
            [
                jnp.sum(
                    jnp.where((lane == sub) & (notes[at, core][0:1] == y.astype(jnp.float32)), 1.0, 0.0),
                    axis=1,
                    keepdims=True,
                )
                for core in range(2)
            ],
            axis=0,
        )
        mean_square = jnp.mean(base * base, axis=-1, keepdims=True)
        normed = (base * (lax.rsqrt(mean_square + 1e-06) * kept) * gain).astype(jnp.bfloat16)
        wide = jnp.dot(normed, up_ref[0], preferred_element_type=jnp.float32)
        wide = 0.5 * wide * (1.0 + jnp.tanh(0.7978845608028654 * (wide + 0.044715 * (wide * wide * wide))))
        hidden = jnp.concatenate(
            [
                wide[source * 128 + target * 16 + core * 8 :][:8]
                for core in range(2)
                for target in range(8)
                for source in range(2)
            ],
            axis=0,
        ).astype(jnp.bfloat16)
        change = jnp.dot(hidden, down_ref[0], preferred_element_type=jnp.float32)
        change = change.astype(jnp.bfloat16)
        parts[at, 0] = change[:128]
        parts[at, 1] = change[128:]
        part(at).start()

    def combine(at):
        part(at).wait_recv()
        both = parts[at, h].astype(jnp.float32) + sibling_parts[at].astype(jnp.float32)
        sums[:, pl.ds(pl.multiple_of(at * 16, 16), 16), :] = both.astype(jnp.bfloat16).reshape(
            8, 16, width
        )

    waiting = []
    for step in range(5):
        ready = []
        if step < 4:
            at = y * 4 + order[step]
            if step > 0:
                await_block(at, h)
            pl.when(has_right & (order[step] <= z))(lambda: send_block(RIGHT, at))
            pl.when(has_left & (order[step] >= z))(lambda: send_block(LEFT, at))
            send_block(ACROSS, at)
            send_block(SIBLING, at)
            ready.append((at, False))
        if step > 0:
            ready.append(((1 - y) * 4 + order[step - 1], True))
        for unit, crossed in ready:
            if crossed:
                await_block(unit, h)
                send_block(SIBLING, unit)
            await_block(unit, 1 - h)
            predict(unit)
            if waiting:
                combine(waiting.pop())
            waiting.append(unit)
    combine(waiting.pop())

    def across(to):
        return remote(
            sums.at[(1 - y) * 4 + to],
            across_parts.at[to],
            across_send.at[to],
            across_recv.at[to],
            ACROSS,
        )

    def along(to, way):
        arrivals, recv = (from_left, left_recv) if way == RIGHT else (from_right, right_recv)
        return remote(
            outgoing.at[to], arrivals.at[to], line_send.at[to], recv.at[to], way
        )

    for step in range(4):
        across(order[3 - step]).start()
    for step in range(3):
        to = order[3 - step]
        across(to).wait_recv()

        def pass_on(way, arrivals, chained):
            def start():
                own = sums[y * 4 + to].astype(jnp.float32) + across_parts[to].astype(jnp.float32)
                outgoing[to] = own.astype(jnp.bfloat16)
                along(to, way).start()

            def go_on():
                along(to, way).wait_recv()
                own = sums[y * 4 + to].astype(jnp.float32) + across_parts[to].astype(jnp.float32)
                outgoing[to] = (own + arrivals[to].astype(jnp.float32)).astype(jnp.bfloat16)
                along(to, way).start()

            pl.when(chained)(go_on)
            pl.when(jnp.logical_not(chained))(start)

        pl.when(to > z)(lambda: pass_on(RIGHT, from_left, has_left))
        pl.when(to < z)(lambda: pass_on(LEFT, from_right, has_right))
    across(z).wait_recv()
    total[...] = sums[chip].astype(jnp.float32) + across_parts[z].astype(jnp.float32)

    @pl.when(has_left)
    def _():
        along(z, RIGHT).wait_recv()
        total[...] += from_left[z].astype(jnp.float32)

    @pl.when(has_right)
    def _():
        along(z, LEFT).wait_recv()
        total[...] += from_right[z].astype(jnp.float32)

    base = rows[:, :, pl.ds(pl.multiple_of(chip * 16, 16), 16), :].astype(jnp.float32)
    base = jnp.where(h == 0, base[:, :, :8], base[:, :, 8:]).reshape(128, width)
    predicted = (base + total[...]).astype(jnp.bfloat16)
    spots = jnp.concatenate(
        [notes[at, core][1:2] for at in range(8) for core in range(2)], axis=0
    ).astype(jnp.bfloat16)
    own_spots = (sub == chip * 16 + h * 8 + (lane & 7)).astype(jnp.bfloat16)
    spread = jnp.dot(spots, own_spots, preferred_element_type=jnp.float32)
    line = lax.broadcasted_iota(jnp.int32, (16, 128), 0)
    across_lanes = lax.broadcasted_iota(jnp.int32, (16, 128), 1)
    spot_row = jnp.sum(
        jnp.where(line == across_lanes >> 3, spread, 0.0), axis=0, keepdims=True
    ).astype(jnp.int32)
    settle = (sub == spot_row).astype(jnp.bfloat16)
    imagined = jnp.dot(settle, predicted, preferred_element_type=jnp.float32)
    imagined_ref[...] = imagined.astype(jnp.bfloat16)
    policy_normed = rms_scale(imagined, policy_gain_ref[...]).astype(jnp.bfloat16)
    action_ref[...] = jnp.tanh(
        jnp.dot(policy_normed, policy_ref[...], preferred_element_type=jnp.float32)
    ).astype(jnp.bfloat16)

    for step in range(4):
        at = y * 4 + order[step]
        other = (1 - y) * 4 + order[step]

        def sent(way, where):
            for copy in block(way, where):
                copy.wait_send()

        pl.when(has_right & (order[step] <= z))(lambda: sent(RIGHT, at))
        pl.when(has_left & (order[step] >= z))(lambda: sent(LEFT, at))
        sent(ACROSS, at)
        sent(SIBLING, at)
        sent(SIBLING, other)
        part(at).wait_send()
        part(other).wait_send()
        across(order[step]).wait_send()
        if step > 0:
            along(order[step], RIGHT).wait_send()


def gathered(states, member_of, place, norm_gain, w_up, w_down, policy_gain, w_policy):
    count, width = states.shape
    vmem = pl.BlockSpec(memory_space=pltpu.VMEM)
    dma = pltpu.SemaphoreType.DMA
    half = jnp.bfloat16
    return pl.pallas_call(
        rollout_kernel,
        out_shape=(
            jax.ShapeDtypeStruct((count, width), half),
            jax.ShapeDtypeStruct((count, w_policy.shape[1]), half),
        ),
        in_specs=[vmem] * 8,
        out_specs=(vmem, vmem),
        scratch_shapes=[
            pltpu.VMEM((8, 2, count, width), half),
            pltpu.VMEM((8, 2, 8, 128), jnp.float32),
            pltpu.VMEM((8, 2, count, width), half),
            pltpu.VMEM((8, count, width), half),
            pltpu.VMEM((8, count, width), half),
            pltpu.VMEM((4, count, width), half),
            pltpu.VMEM((4, count, width), half),
            pltpu.VMEM((4, count, width), half),
            pltpu.VMEM((4, count, width), half),
            pltpu.VMEM((count, width), jnp.float32),
            dma((2, 4, 8)),
            dma((2, 8, 2)),
            dma((8,)),
            dma((8,)),
            dma((4,)),
            dma((4,)),
            dma((4,)),
            dma((4,)),
            dma((4,)),
        ],
        compiler_params=pltpu.CompilerParams(
            collective_id=0, has_side_effects=True, vmem_limit_bytes=48 * 1024 * 1024
        ),
        cost_estimate=pl.CostEstimate(
            flops=2 * 2 * 16 * count * width * w_up.shape[2],
            bytes_accessed=8 * 1024 * 1024,
            transcendentals=16 * count * w_up.shape[2],
        ),
    )(
        states,
        member_of,
        place.reshape(1, count),
        norm_gain,
        w_up,
        w_down,
        policy_gain.reshape(1, width),
        w_policy,
    )


def solution(mesh):
    in_specs = (
        P(("rep", "member", "tp"), None),
        P(("rep", "member", "tp"), None),
        P(("rep", "member", "tp")),
        P(),
        P("member", None, "tp"),
        P("member", "tp", None),
        P(),
        P(),
    )
    out_specs = (P(("rep", "member", "tp"), None), P(("rep", "member", "tp"), None))
    local = gathered if mesh.shape["member"] == 4 and mesh.shape["tp"] == 4 else dispatched
    return jax.shard_map(local, mesh=mesh, in_specs=in_specs, out_specs=out_specs, check_vma=False)
```

```python
import jax
import jax.numpy as jnp
from jax import lax
from jax.experimental import pallas as pl
from jax.experimental.pallas import tpu as pltpu
from jax.sharding import PartitionSpec as P


def from_partner(value, axis, distance):
    return lax.ppermute(value, axis, [(i, i ^ 1 << distance) for i in range(lax.axis_size(axis))])


def rms_scale(values, gain):
    mean_square = jnp.mean(values * values, axis=-1, keepdims=True)
    return values * lax.rsqrt(mean_square + 1e-06) * gain


def running_rank(member_hits):
    return jnp.sum((jnp.cumsum(member_hits, axis=0) - member_hits) * member_hits, axis=1)


def dispatched(states, member_of, place, norm_gain, w_up, w_down, policy_gain, w_policy):
    n_member = lax.axis_size("member")
    n_tp = lax.axis_size("tp")
    n_dev = n_member * n_tp
    group_width = 2 * n_tp
    member_total = n_member // 2
    rows_here = states.shape[0]
    feature_width = states.shape[1]
    slot_count = 2 * rows_here // n_dev
    member = member_of[:, 0]
    member_hits = (member[:, None] == jnp.arange(member_total, dtype=jnp.int32)[None, :]).astype(
        jnp.int32
    )
    earlier = running_rank(member_hits)
    target = (member * group_width + earlier % group_width) * slot_count + earlier // group_width
    picker = (jnp.arange(n_dev * slot_count, dtype=jnp.int32)[:, None] == target[None, :]).astype(
        jnp.bfloat16
    )
    outgoing = jnp.dot(picker, states, preferred_element_type=jnp.float32).astype(jnp.bfloat16)
    arrived = lax.all_to_all(
        outgoing.reshape(n_dev, slot_count, feature_width),
        ("member", "tp"),
        split_axis=0,
        concat_axis=0,
        tiled=True,
    )
    arrived = arrived.reshape(n_dev * slot_count, feature_width)
    arrived_count = arrived.shape[0]
    own_member = lax.axis_index("member") // 2
    gain_here = lax.dynamic_index_in_dim(norm_gain, own_member, 0, keepdims=False)
    normed = rms_scale(arrived.astype(jnp.float32), gain_here).astype(jnp.bfloat16)
    partner_normed = from_partner(normed, "member", 0)
    both_rows = jnp.concatenate([normed, partner_normed], axis=0)
    up_local = w_up[0]
    down_local = w_down[0]
    hidden = jax.nn.gelu(
        jnp.dot(
            lax.all_gather(both_rows, "tp", axis=0, tiled=True),
            up_local,
            preferred_element_type=jnp.float32,
        )
    ).astype(jnp.bfloat16)
    half_change = lax.psum_scatter(
        jnp.dot(hidden, down_local, preferred_element_type=jnp.float32),
        "tp",
        scatter_dimension=0,
        tiled=True,
    )
    partner_part = from_partner(half_change[arrived_count:], "member", 0)
    change = half_change[:arrived_count] + partner_part
    predicted = (arrived.astype(jnp.float32) + change).astype(jnp.bfloat16)
    returned = lax.all_to_all(
        predicted.reshape(n_dev, slot_count, feature_width),
        ("member", "tp"),
        split_axis=0,
        concat_axis=0,
        tiled=True,
    )
    returned = returned.reshape(n_dev * slot_count, feature_width)
    own_rows = jnp.einsum("sr,sd->rd", picker, returned, preferred_element_type=jnp.float32).astype(
        jnp.bfloat16
    )
    per_learner = rows_here // n_dev
    learner = place // rows_here
    spot_index = place % rows_here
    learner_hits = (learner[:, None] == jnp.arange(n_dev, dtype=jnp.int32)[None, :]).astype(
        jnp.int32
    )
    lane_index = learner * per_learner + running_rank(learner_hits)
    placer = jnp.arange(rows_here, dtype=jnp.int32)[:, None] == lane_index[None, :]
    packed = jnp.dot(
        placer.astype(jnp.bfloat16), own_rows, preferred_element_type=jnp.float32
    ).astype(jnp.bfloat16)
    packed_spot = jnp.sum(placer.astype(jnp.int32) * spot_index[None, :], axis=1)
    arrivals, arrival_spots = (
        lax.all_to_all(
            packed.reshape(n_dev, per_learner, feature_width),
            ("member", "tp"),
            split_axis=0,
            concat_axis=0,
            tiled=True,
        ),
        lax.all_to_all(
            packed_spot.reshape(n_dev, per_learner),
            ("member", "tp"),
            split_axis=0,
            concat_axis=0,
            tiled=True,
        ),
    )
    arrivals = arrivals.reshape(rows_here, feature_width)
    arrival_spots = arrival_spots.reshape(rows_here)
    settle = (jnp.arange(rows_here, dtype=jnp.int32)[:, None] == arrival_spots[None, :]).astype(
        jnp.bfloat16
    )
    imagined = jnp.dot(settle, arrivals, preferred_element_type=jnp.float32).astype(jnp.bfloat16)
    policy_normed = rms_scale(imagined.astype(jnp.float32), policy_gain).astype(jnp.bfloat16)
    action = jnp.tanh(jnp.dot(policy_normed, w_policy, preferred_element_type=jnp.float32)).astype(
        jnp.bfloat16
    )
    return (imagined, action)


RIGHT, LEFT, ACROSS, SIBLING = range(4)


def near_order(z):
    return (
        z,
        z - 1 + 2 * ((3 - z) // 3),
        2 + z // 2 - 2 * (z // 3),
        3 - 3 * (z // 2),
    )


def rollout_kernel(
    states_in,
    member_in,
    place_in,
    gain_in,
    up_in,
    down_in,
    policy_gain_in,
    policy_in,
    imagined_ref,
    action_ref,
    states_ref,
    member_ref,
    place_ref,
    gain_ref,
    up_ref,
    down_ref,
    policy_gain_ref,
    policy_ref,
    fetch_sem,
    rows,
    notes,
    parts,
    sibling_parts,
    sums,
    across_parts,
    from_left,
    from_right,
    outgoing,
    total,
    gather_send,
    gather_recv,
    part_send,
    part_recv,
    across_send,
    across_recv,
    line_send,
    left_recv,
    right_recv,
):
    width = states_ref.shape[1]
    fetches = [
        pltpu.make_async_copy(source, target, fetch_sem.at[i])
        for i, (source, target) in enumerate(
            (
                (place_in, place_ref),
                (member_in, member_ref),
                (states_in, states_ref),
                (gain_in, gain_ref),
                (up_in, up_ref),
                (down_in, down_ref),
                (policy_gain_in, policy_gain_ref),
                (policy_in, policy_ref),
            )
        )
    ]
    for fetch in fetches:
        fetch.start()
    z = lax.axis_index("tp")
    m = lax.axis_index("member")
    y = m // 2
    h = m % 2
    chip = y * 4 + z
    targets = {
        RIGHT: {"tp": z + 1},
        LEFT: {"tp": z - 1},
        ACROSS: {"member": m + 2 - 4 * y},
        SIBLING: {"member": m + 1 - 2 * h},
    }
    has_right = z < 3
    has_left = z > 0
    order = near_order(z)

    def greet(way):
        pl.semaphore_signal(
            barrier, inc=1, device_id=targets[way], device_id_type=pl.DeviceIdType.MESH
        )

    def remote(source, target, send_sem, recv_sem, way):
        return pltpu.make_async_remote_copy(
            src_ref=source,
            dst_ref=target,
            send_sem=send_sem,
            recv_sem=recv_sem,
            device_id=targets[way],
            device_id_type=pl.DeviceIdType.MESH,
        )

    barrier = pltpu.get_barrier_semaphore()
    greet(ACROSS)
    greet(SIBLING)
    pl.when(has_right)(lambda: greet(RIGHT))
    pl.when(has_left)(lambda: greet(LEFT))

    for fetch in fetches[:3]:
        fetch.wait()
    lane = lax.broadcasted_iota(jnp.int32, (128, 128), 1)
    sub = lax.broadcasted_iota(jnp.int32, (128, 128), 0)
    place_row = place_ref[...]
    learner = place_row >> 7
    spot = place_row & 127
    key_row = ((((learner >> 3) << 2) + (learner & 3)) << 1) + ((learner >> 2) & 1)
    rank_row = key_row * 128 + lax.broadcasted_iota(jnp.int32, (1, 128), 1)
    rank_col = jnp.sum(jnp.where(lane == sub, rank_row, 0), axis=1, keepdims=True)
    sorted_row = jnp.sum((rank_col < rank_row).astype(jnp.int32), axis=0, keepdims=True)
    picker = (sub == sorted_row).astype(jnp.bfloat16)
    member_row = jnp.sum(jnp.where(lane == sub, member_ref[...], 0), axis=0, keepdims=True)
    line = lax.broadcasted_iota(jnp.int32, (16, 128), 0)
    facts = jnp.where(line == 0, member_row, jnp.where(line == 1, spot, 0))
    own_notes = lax.dot_general(
        facts.astype(jnp.bfloat16),
        picker,
        (((1,), (1,)), ((), ())),
        preferred_element_type=jnp.float32,
    )
    notes[chip, h] = own_notes[:8]
    rows[chip, h] = jnp.dot(
        picker, states_ref[...], preferred_element_type=jnp.float32
    ).astype(jnp.bfloat16)

    pl.semaphore_wait(barrier, 2 + (z + 2) // 3 + (5 - z) // 3)

    def pieces(at, core):
        return (
            notes.at[at, core],
            rows.at[at, core, pl.ds(0, 64)],
            rows.at[at, core, pl.ds(64, 64)],
        )

    def piece(way, at, kind):
        where = pieces(at, h)[kind]
        return remote(
            where, where, gather_send.at[kind, way, at], gather_recv.at[kind, at, h], way
        )

    def await_piece(at, core, kind):
        where = pieces(at, core)[kind]
        remote(
            where,
            where,
            gather_send.at[kind, SIBLING, at],
            gather_recv.at[kind, at, core],
            SIBLING,
        ).wait_recv()

    def part(at):
        return remote(
            parts.at[at, 1 - h],
            sibling_parts.at[at],
            part_send.at[at],
            part_recv.at[at],
            SIBLING,
        )

    def predict(at):
        base = jnp.concatenate([rows[at, 0], rows[at, 1]], axis=0).astype(jnp.float32)
        kept = jnp.concatenate(
            [
                jnp.sum(
                    jnp.where((lane == sub) & (notes[at, core][0:1] == y.astype(jnp.float32)), 1.0, 0.0),
                    axis=1,
                    keepdims=True,
                )
                for core in range(2)
            ],
            axis=0,
        )
        mean_square = jnp.mean(base * base, axis=-1, keepdims=True)
        normed = (base * (lax.rsqrt(mean_square + 1e-06) * kept) * gain).astype(jnp.bfloat16)
        wide = jnp.dot(normed, up_ref[0], preferred_element_type=jnp.float32)
        wide = 0.5 * wide * (1.0 + jnp.tanh(0.7978845608028654 * (wide + 0.044715 * (wide * wide * wide))))
        hidden = jnp.concatenate(
            [
                wide[source * 128 + target * 16 + core * 8 :][:8]
                for core in range(2)
                for target in range(8)
                for source in range(2)
            ],
            axis=0,
        ).astype(jnp.bfloat16)
        change = jnp.dot(hidden, down_ref[0], preferred_element_type=jnp.float32)
        change = change.astype(jnp.bfloat16)
        parts[at, 0] = change[:128]
        parts[at, 1] = change[128:]
        part(at).start()

    def combine(at):
        part(at).wait_recv()
        both = parts[at, h].astype(jnp.float32) + sibling_parts[at].astype(jnp.float32)
        sums[:, pl.ds(pl.multiple_of(at * 16, 16), 16), :] = both.astype(jnp.bfloat16).reshape(
            8, 16, width
        )

    def across(to, line):
        span = pl.ds(pl.multiple_of(line * 64, 64), 64)
        return remote(
            sums.at[(1 - y) * 4 + to, span],
            across_parts.at[to, span],
            across_send.at[to, line],
            across_recv.at[to, line],
            ACROSS,
        )

    for fetch in fetches[3:6]:
        fetch.wait()
    gain = gain_ref[pl.ds(y, 1), :]
    waiting = []
    for step in range(5):
        if step < 4:
            at = y * 4 + order[step]
            for kind in range(3):
                if step > 0:
                    await_piece(at, h, kind)
                pl.when(has_right & (order[step] <= z))(lambda: piece(RIGHT, at, kind).start())
                pl.when(has_left & (order[step] >= z))(lambda: piece(LEFT, at, kind).start())
                piece(ACROSS, at, kind).start()
                piece(SIBLING, at, kind).start()
            for kind in range(3):
                await_piece(at, 1 - h, kind)
            predict(at)
            waiting.append(at)
        if step > 0:
            crossed = (1 - y) * 4 + order[step - 1]
            for kind in range(3):
                await_piece(crossed, h, kind)
                piece(SIBLING, crossed, kind).start()
            while waiting:
                combine(waiting.pop(0))
            if step == 3:
                for k in range(4):
                    across(order[3 - k], y).start()
            for kind in range(3):
                await_piece(crossed, 1 - h, kind)
            predict(crossed)
            waiting.append(crossed)
    combine(waiting.pop())

    def along(to, line, way):
        span = pl.ds(pl.multiple_of(line * 64, 64), 64)
        arrivals, recv = (from_left, left_recv) if way == RIGHT else (from_right, right_recv)
        return remote(
            outgoing.at[to, span],
            arrivals.at[to, span],
            line_send.at[to, line],
            recv.at[to, line],
            way,
        )

    for k in range(2):
        across(order[3 - k], 1 - y).start()
    for turn, line in enumerate((1 - y, y)):
        span = pl.ds(pl.multiple_of(line * 64, 64), 64)
        for k in range(3):
            to = order[3 - k]
            across(to, line).wait_recv()

            def pass_on(way, arrivals, chained):
                def summed():
                    own = sums[y * 4 + to, span].astype(jnp.float32)
                    return own + across_parts[to, span].astype(jnp.float32)

                def start():
                    outgoing[to, span] = summed().astype(jnp.bfloat16)
                    along(to, line, way).start()

                def go_on():
                    along(to, line, way).wait_recv()
                    both = summed() + arrivals[to, span].astype(jnp.float32)
                    outgoing[to, span] = both.astype(jnp.bfloat16)
                    along(to, line, way).start()

                pl.when(chained)(go_on)
                pl.when(jnp.logical_not(chained))(start)

            pl.when(to > z)(lambda: pass_on(RIGHT, from_left, has_left))
            pl.when(to < z)(lambda: pass_on(LEFT, from_right, has_right))
            if turn == 0 and k < 2:
                across(order[3 - k], 1 - y).wait_send()
                across(order[1 - k], 1 - y).start()
        across(z, line).wait_recv()
        total[span] = sums[chip, span].astype(jnp.float32) + across_parts[z, span].astype(
            jnp.float32
        )

        @pl.when(has_left)
        def _():
            along(z, line, RIGHT).wait_recv()
            total[span] += from_left[z, span].astype(jnp.float32)

        @pl.when(has_right)
        def _():
            along(z, line, LEFT).wait_recv()
            total[span] += from_right[z, span].astype(jnp.float32)

    for fetch in fetches[6:]:
        fetch.wait()
    base = rows[:, :, pl.ds(pl.multiple_of(chip * 16, 16), 16), :].astype(jnp.float32)
    base = jnp.where(h == 0, base[:, :, :8], base[:, :, 8:]).reshape(128, width)
    predicted = (base + total[...]).astype(jnp.bfloat16)
    spots = jnp.concatenate(
        [notes[at, core][1:2] for at in range(8) for core in range(2)], axis=0
    ).astype(jnp.bfloat16)
    own_spots = (sub == chip * 16 + h * 8 + (lane & 7)).astype(jnp.bfloat16)
    spread = jnp.dot(spots, own_spots, preferred_element_type=jnp.float32)
    line = lax.broadcasted_iota(jnp.int32, (16, 128), 0)
    across_lanes = lax.broadcasted_iota(jnp.int32, (16, 128), 1)
    spot_row = jnp.sum(
        jnp.where(line == across_lanes >> 3, spread, 0.0), axis=0, keepdims=True
    ).astype(jnp.int32)
    settle = (sub == spot_row).astype(jnp.bfloat16)
    imagined = jnp.dot(settle, predicted, preferred_element_type=jnp.float32)
    imagined_ref[...] = imagined.astype(jnp.bfloat16)
    policy_normed = rms_scale(imagined, policy_gain_ref[...]).astype(jnp.bfloat16)
    action_ref[...] = jnp.tanh(
        jnp.dot(policy_normed, policy_ref[...], preferred_element_type=jnp.float32)
    ).astype(jnp.bfloat16)

    for step in range(4):
        at = y * 4 + order[step]
        other = (1 - y) * 4 + order[step]

        for kind in range(3):
            pl.when(has_right & (order[step] <= z))(lambda: piece(RIGHT, at, kind).wait_send())
            pl.when(has_left & (order[step] >= z))(lambda: piece(LEFT, at, kind).wait_send())
            piece(ACROSS, at, kind).wait_send()
            piece(SIBLING, at, kind).wait_send()
            piece(SIBLING, other, kind).wait_send()
        part(at).wait_send()
        part(other).wait_send()
        across(order[step], y).wait_send()
        if step < 2:
            across(order[step], 1 - y).wait_send()
        if step > 0:
            for line in range(2):
                along(order[step], line, RIGHT).wait_send()


def gathered(states, member_of, place, norm_gain, w_up, w_down, policy_gain, w_policy):
    count, width = states.shape
    vmem = pl.BlockSpec(memory_space=pltpu.VMEM)
    dma = pltpu.SemaphoreType.DMA
    half = jnp.bfloat16
    operands = (
        states,
        member_of,
        place.reshape(1, count),
        norm_gain,
        w_up,
        w_down,
        policy_gain.reshape(1, width),
        w_policy,
    )
    return pl.pallas_call(
        rollout_kernel,
        out_shape=(
            jax.ShapeDtypeStruct((count, width), half),
            jax.ShapeDtypeStruct((count, w_policy.shape[1]), half),
        ),
        in_specs=[pl.BlockSpec(memory_space=pltpu.HBM)] * 8,
        out_specs=(vmem, vmem),
        scratch_shapes=[
            *(pltpu.VMEM(operand.shape, operand.dtype) for operand in operands),
            dma((8,)),
            pltpu.VMEM((8, 2, count, width), half),
            pltpu.VMEM((8, 2, 8, 128), jnp.float32),
            pltpu.VMEM((8, 2, count, width), half),
            pltpu.VMEM((8, count, width), half),
            pltpu.VMEM((8, count, width), half),
            pltpu.VMEM((4, count, width), half),
            pltpu.VMEM((4, count, width), half),
            pltpu.VMEM((4, count, width), half),
            pltpu.VMEM((4, count, width), half),
            pltpu.VMEM((count, width), jnp.float32),
            dma((3, 4, 8)),
            dma((3, 8, 2)),
            dma((8,)),
            dma((8,)),
            dma((4, 2)),
            dma((4, 2)),
            dma((4, 2)),
            dma((4, 2)),
            dma((4, 2)),
        ],
        compiler_params=pltpu.CompilerParams(
            collective_id=0, has_side_effects=True, vmem_limit_bytes=48 * 1024 * 1024
        ),
        cost_estimate=pl.CostEstimate(
            flops=2 * 2 * 16 * count * width * w_up.shape[2],
            bytes_accessed=8 * 1024 * 1024,
            transcendentals=16 * count * w_up.shape[2],
        ),
    )(*operands)


def solution(mesh):
    in_specs = (
        P(("rep", "member", "tp"), None),
        P(("rep", "member", "tp"), None),
        P(("rep", "member", "tp")),
        P(),
        P("member", None, "tp"),
        P("member", "tp", None),
        P(),
        P(),
    )
    out_specs = (P(("rep", "member", "tp"), None), P(("rep", "member", "tp"), None))
    local = gathered if mesh.shape["member"] == 4 and mesh.shape["tp"] == 4 else dispatched
    return jax.shard_map(local, mesh=mesh, in_specs=in_specs, out_specs=out_specs, check_vma=False)
```
